32 devices in a mesh: visit: 4 (over z), patch: 8 (over y, x, core).
Axes of the slice: x: 2, y: 2, z: 4, core: 2. Of those that a mesh axis runs over, the one named last changes fastest.
Arguments:
- ccd_images: bfloat16 [128, 512, 256], P(('visit', 'patch')), may hold values from -6 to 6
- ccd_weight: float32 [128], replicated, may hold values from 0.25 to 4
- psf_index: int32 [128], replicated, may hold values from 0 to 7
- patch_target: int32 [512, 1], replicated, may hold values from 0 to 7; in each aligned block of 16 rows (0 to 15, 16 to 31, ...) at most 2 rows name the same one
- tile_slot: int32 [512], replicated, may hold values from 0 to 15
- row_matrix: int32 [512], replicated, may hold values from 0 to 7
- col_matrix: int32 [512], replicated, may hold values from 0 to 7
- warp_rows: bfloat16 [8, 256, 512], replicated, may hold values from -0.25 to 0.25
- warp_cols: bfloat16 [8, 256, 256], replicated, may hold values from -0.375 to 0.375
- psf_match: bfloat16 [8, 256, 256], replicated, may hold values from -0.375 to 0.375
- detect_kernel: float32 [9], replicated, may hold values from 0.2 to 1
Outputs:
- coadd: float32 [1024, 8192], P('visit', 'patch')
- detection: float32 [1024, 8192], P('visit', 'patch')
The draws below stay inside these ranges and needn't reach their ends.
Inputs may be any that keep to these rules, and one draw needn't show every extreme that they name: `patch_target`: in each aligned block of 16 entries (the entries of one device) no patch is named more than 2 times, a bound that some block reaches.
All inputs are finite; a program needn't handle non-finite values.
Results may differ from the reference program's by a relative error of at most 0.0057.
Values may be sent and summed in bfloat16 or wider, within the bound.
A program may use at most 128 MiB of HBM per device.

```python
import math
import jax
import jax.numpy as jnp
import numpy as np
from jax import lax

CCD_DEV = 4
CH = 512
CW = 256
K_OV = 4
TS = 256
G = 4
CAP = 2
NW = 8
NPSF = 8
RADIUS = 4
NCCD = 128
NENT = 512
KLEN = 9
N_PATCH = 8


def with_ends(array, own_key, low, top_value):
    longest = array.shape.index(max(array.shape))
    spots = []
    for shift in (0, 1):
        where = [jax.random.randint(jax.random.fold_in(own_key, axis), (), 0, length) for axis, length in enumerate(array.shape)]
        where[longest] = (where[longest] + shift) % array.shape[longest]
        spots.append(tuple(where))
    return array.at[spots[0]].set(low).at[spots[1]].set(top_value)


def level_of(own_key, dims, split, least, high):
    def one(dim, parts):
        draws = jax.random.uniform(jax.random.fold_in(jax.random.fold_in(own_key, 6), dim), (parts,), jnp.float32, least / len(split), high / len(split))
        return jnp.repeat(jnp.exp(draws), dims[dim] // parts).reshape((-1,) + (1,) * (len(dims) - dim - 1))

    level = one(*split[0])
    for cut in split[1:]:
        level = level * one(*cut)
    return level


def shared_out(rng, own, number, rows, number_of, top, most, skew):
    sequence = jax.random.permutation(rng, number_of)
    crowded, ordinary = load_shares(number_of, rows * top, most, skew, True), load_shares(number_of, rows * top, most, skew, False)
    places = jnp.arange(number_of)

    def named(tallies, turn):
        used = int((tallies > 0).sum())
        fixed = max(1, used // 4)
        moved = fixed + (places - fixed + turn * (used - fixed)) % max(1, number_of - fixed)
        return jnp.zeros((number_of,), jnp.int32).at[sequence[jnp.where(places < fixed, places, moved)]].set(jnp.asarray(tallies, jnp.int32))

    tallies = jnp.where(number % 4 == 0, named(crowded, number // 4), named(ordinary, number - number // 4 - 1))
    mixed = jax.random.permutation(jax.random.fold_in(own, 3), number_of)
    giver, taker = mixed[0:number_of // 2 * 2:2], mixed[1:number_of // 2 * 2:2]
    room = jnp.minimum(tallies[giver] - 1, most - tallies[taker]) // 2
    room = jnp.where((giver == sequence[0]) | (taker == sequence[0]) | (tallies[taker] == 0), 0, jnp.maximum(room, 0))
    moved = jax.random.randint(jax.random.fold_in(own, 4), (number_of // 2,), 0, 1 << 20) % (room + 1)
    tallies = tallies.at[giver].add(-moved).at[taker].add(moved)
    members = jnp.searchsorted(jnp.cumsum(tallies), jnp.arange(rows * top), side="right").astype(jnp.int32)
    grid = members.reshape(top, rows).T
    grid = grid[jax.random.permutation(jax.random.fold_in(own, 1), rows)]
    turn = jax.random.randint(jax.random.fold_in(own, 2), (rows, 1), 0, top)
    return jnp.take_along_axis(grid, (jnp.arange(top)[None, :] + turn) % top, axis=1)


def load_shares(number_of, total, reach, slope, full):
    weights = [(1 << 20) // math.isqrt(standing ** slope) + 1 for standing in range(1, number_of + 1)]
    largest = reach if full else min(reach, max(-(-total // number_of), total * weights[0] // sum(weights)))
    least = 1 if total - largest >= number_of - 1 else 0
    holding, spare = [largest] + [least] * (number_of - 1), total - largest - least * (number_of - 1)
    while spare > 0:
        free = [i for i in range(1, number_of) if holding[i] < largest] or [i for i in range(1, number_of) if holding[i] < reach]
        mass, remaining = sum([weights[i] for i in free]), spare
        for i in free:
            extra = min(reach - holding[i], max(1, remaining * weights[i] // mass), spare)
            holding[i] = holding[i] + extra
            spare = spare - extra
    return np.array(holding)


def noise(stream_key, extent, spread, bound, split=(), held_as=jnp.bfloat16):
    drawn = jax.random.normal(stream_key, extent, jnp.float32) * spread
    if len(split) > 0:
        drawn = level_of(stream_key, extent, split, -0.22, 0.18) * drawn
    return jnp.clip(drawn, min=-bound, max=bound).astype(held_as)


def setup_inputs(seed: int = 0) -> dict:
    key_of = jax.random.split(jax.random.key(seed), 12)
    ccd_images = noise(key_of[0], (NCCD, CH, CW), 1.0, 6.0, ((0, 32),))
    ccd_weight = jnp.clip(jnp.exp(jax.random.uniform(key_of[1], (NCCD,), jnp.float32, math.log(0.25), math.log(4.0))), 0.25, 4.0)
    psf_index = with_ends(jax.random.randint(key_of[2], (NCCD,), 0, NPSF), jax.random.fold_in(key_of[2], 1), 0, NPSF - 1).astype(jnp.int32)
    patch_target_keys = jax.random.split(jax.random.fold_in(key_of[3], 1), NENT // (CCD_DEV * K_OV))
    patch_target_turns = jax.random.permutation(jax.random.fold_in(key_of[3], 3), NENT // (CCD_DEV * K_OV))
    patch_target = jax.vmap(lambda own, number: shared_out(jax.random.fold_in(key_of[3], 2), own, number, CCD_DEV * K_OV, N_PATCH, 1, CAP, 2))(patch_target_keys, patch_target_turns).reshape((NENT, 1))
    tile_slot = with_ends(jax.random.randint(key_of[4], (NENT,), 0, G * G), jax.random.fold_in(key_of[4], 1), 0, (G * G) - 1).astype(jnp.int32)
    row_matrix = with_ends(jax.random.randint(key_of[5], (NENT,), 0, NW), jax.random.fold_in(key_of[5], 1), 0, NW - 1).astype(jnp.int32)
    col_matrix = with_ends(jax.random.randint(key_of[6], (NENT,), 0, NW), jax.random.fold_in(key_of[6], 1), 0, NW - 1).astype(jnp.int32)
    warp_rows = noise(key_of[7], (NW, TS, CH), CH ** -0.5, 0.25)
    warp_cols = noise(key_of[8], (NW, TS, CW), CW ** -0.5, 0.375)
    psf_match = noise(key_of[9], (NPSF, TS, TS), TS ** -0.5, 0.375)
    detect_kernel = jnp.clip(jax.random.uniform(key_of[10], (KLEN,), jnp.float32, 0.2, 1.0), 0.2, 1.0)
    return dict(ccd_images=ccd_images, ccd_weight=ccd_weight, psf_index=psf_index, patch_target=patch_target, tile_slot=tile_slot, row_matrix=row_matrix, col_matrix=col_matrix, warp_rows=warp_rows, warp_cols=warp_cols, psf_match=psf_match, detect_kernel=detect_kernel)


def warp_entries(images, row_tables, col_tables, psf_tables):
    first = jnp.einsum('ntc,ncw->ntw', row_tables.astype(jnp.float32), images.astype(jnp.float32)).astype(jnp.bfloat16)
    second = jnp.einsum('ntw,nuw->ntu', first.astype(jnp.float32), col_tables.astype(jnp.float32)).astype(jnp.bfloat16)
    third = jnp.einsum('nst,ntu->nsu', psf_tables.astype(jnp.float32), second.astype(jnp.float32)).astype(jnp.bfloat16)
    return jnp.einsum('nsu,nvu->nsv', third.astype(jnp.float32), psf_tables.astype(jnp.float32)).astype(jnp.bfloat16)


def reference(ccd_images, ccd_weight, psf_index, patch_target, tile_slot, row_matrix, col_matrix, warp_rows, warp_cols, psf_match, detect_kernel):
    def per_image(packed):
        image, row_pick, col_pick, psf_pick = packed
        images = jnp.broadcast_to(image[None], (K_OV, CH, CW))
        psf_tables = jnp.broadcast_to(psf_match[psf_pick][None], (K_OV, TS, TS))
        return warp_entries(images, warp_rows[row_pick], warp_cols[col_pick], psf_tables)

    tiles = lax.map(per_image, (ccd_images, row_matrix.reshape(NCCD, K_OV), col_matrix.reshape(NCCD, K_OV), psf_index))
    tiles = tiles.reshape(NENT, TS, TS)
    weights = jnp.repeat(ccd_weight, K_OV)
    keys = (patch_target[:, 0] * (G * G) + tile_slot).astype(jnp.int32)
    numerator = jax.ops.segment_sum(weights[:, None, None] * tiles.astype(jnp.float32), keys, num_segments=N_PATCH * G * G)
    weight_sum = jax.ops.segment_sum(weights, keys, num_segments=N_PATCH * G * G)
    image_num = numerator.reshape(N_PATCH, G, G, TS, TS).transpose(1, 3, 0, 2, 4).reshape(G * TS, N_PATCH * G * TS)
    weight_grid = weight_sum.reshape(N_PATCH, G, G).transpose(1, 0, 2)[:, None, :, :, None]
    image_weight = jnp.broadcast_to(weight_grid, (G, TS, N_PATCH, G, TS)).reshape(G * TS, N_PATCH * G * TS)
    coadd = image_num / (1.0 + image_weight)
    height = G * TS
    width = N_PATCH * G * TS
    padded = jnp.pad(coadd, RADIUS)
    row_pass = detect_kernel[0] * padded[0:height, :]
    for offset in range(1, 2 * RADIUS + 1):
        row_pass = row_pass + detect_kernel[offset] * padded[offset:offset + height, :]
    detection = detect_kernel[0] * row_pass[:, 0:width]
    for offset in range(1, 2 * RADIUS + 1):
        detection = detection + detect_kernel[offset] * row_pass[:, offset:offset + width]
    return coadd, detection
```

```python
import functools

import jax
import jax.numpy as jnp
from jax import lax
from jax.experimental import pallas as pl
from jax.experimental.pallas import tpu as pltpu
from jax.sharding import PartitionSpec as P

K_OV = 4
TS = 256
G = 4
CAP = 2
STEPS = 4
BAND = 16
EDGE_R = 8
EDGE_C = 128
MESH = pl.DeviceIdType.MESH
F32 = jnp.float32
BF16 = jnp.bfloat16
NT = (((1,), (1,)), ((), ()))


def kernel(
    n_visit,
    n_patch,
    images,
    row_tables,
    col_tables,
    psf_tables,
    taps,
    weight,
    psf_index,
    target,
    slot,
    row_pick,
    col_pick,
    target_v,
    slot_v,
    weight_v,
    coadd,
    detection,
    second,
    psf_of,
    outbox,
    inbox,
    sums,
    arrived,
    mix_hi,
    mix_lo,
    ext,
    p_send,
    p_recv,
    v_send,
    v_recv,
    h_send,
    h_recv,
):
    v = lax.axis_index("visit")
    p = lax.axis_index("patch")
    per_device = images.shape[0] * K_OV
    boxes = n_patch * CAP
    rows = coadd.shape[0]
    width = coadd.shape[1]
    step_rows = rows // STEPS
    parts = TS // rows
    base = (v * n_patch + p) * per_device

    def entry_for(start, patch, rank):
        seen = jnp.int32(0)
        found = jnp.int32(0)
        filled = jnp.int32(0)
        for e in range(per_device):
            hit = target[start + e] == patch
            take = jnp.logical_and(hit, seen == rank)
            found = jnp.where(take, e, found)
            filled = jnp.where(take, 1, filled)
            seen = seen + hit.astype(jnp.int32)
        return found, filled

    ext[...] = jnp.zeros_like(ext)
    barrier = pltpu.get_barrier_semaphore()
    for d in range(1, n_patch):
        pl.semaphore_signal(
            barrier, inc=1, device_id=(v, lax.rem(p + d, n_patch)), device_id_type=MESH
        )
    for d in range(1, n_visit):
        pl.semaphore_signal(
            barrier, inc=1, device_id=(lax.rem(v + d, n_visit), p), device_id_type=MESH
        )
    corners = [(dv, dp) for dv in (-1, 1) for dp in (-1, 1)]
    sides = [(-1, 0), (1, 0), (0, -1), (0, 1)]

    def inside(dv, dp):
        ok = None
        for at, shift, count in ((v, dv, n_visit), (p, dp, n_patch)):
            if shift < 0:
                term = at > 0
            elif shift > 0:
                term = at < count - 1
            else:
                continue
            ok = term if ok is None else jnp.logical_and(ok, term)
        return ok

    for dv, dp in corners:
        there = (lax.rem(v + dv + n_visit, n_visit), lax.rem(p + dp + n_patch, n_patch))
        pl.semaphore_signal(barrier, inc=1, device_id=there, device_id_type=MESH)

    def warp(s, _):
        entry, _filled = entry_for(base, s // CAP, lax.rem(s, CAP))
        image = images[entry // K_OV]
        first = jnp.dot(
            row_tables[row_pick[base + entry]], image, preferred_element_type=F32
        ).astype(BF16)
        second[s] = lax.dot_general(
            first, col_tables[col_pick[base + entry]], NT, preferred_element_type=F32
        ).astype(BF16)
        psf_of[s] = psf_index[(base + entry) // K_OV]
        return 0

    lax.fori_loop(0, boxes, warp, 0)

    def match(c):
        def one(s, _):
            table = psf_tables[psf_of[s]]
            for h in range(parts):
                at = pl.multiple_of(h * rows + c * step_rows, step_rows)
                left = psf_tables[psf_of[s], pl.ds(at, step_rows), :]
                third = jnp.dot(left, second[s], preferred_element_type=F32).astype(BF16)
                outbox[c, s, h * step_rows : (h + 1) * step_rows, :] = lax.dot_general(
                    third, table, NT, preferred_element_type=F32
                ).astype(BF16)
            return 0

        lax.fori_loop(0, boxes, one, 0)

    def patch_copy(c, d):
        there = lax.rem(p + d, n_patch)
        return pltpu.make_async_remote_copy(
            src_ref=outbox.at[c, pl.ds(there * CAP, CAP)],
            dst_ref=inbox.at[c, pl.ds(p * CAP, CAP)],
            send_sem=p_send.at[c, d - 1],
            recv_sem=p_recv.at[c, d - 1],
            device_id=(v, there),
            device_id_type=MESH,
        )

    def visit_copy(c, d):
        there = lax.rem(v + d, n_visit)
        return pltpu.make_async_remote_copy(
            src_ref=sums.at[c, there],
            dst_ref=arrived.at[c, d - 1],
            send_sem=v_send.at[c, d - 1],
            recv_sem=v_recv.at[c, d - 1],
            device_id=(there, p),
            device_id_type=MESH,
        )

    def send_patch(c):
        for d in range(1, n_patch):
            patch_copy(c, d).start()
        inbox[c, pl.ds(p * CAP, CAP)] = outbox[c, pl.ds(p * CAP, CAP)]

    def combine(c):
        for d in range(1, n_patch):
            patch_copy(c, d).wait_recv()
        for h in range(parts):

            def band(i, _):
                at = pl.multiple_of(h * step_rows + i * BAND, BAND)
                tiles = inbox[c, :, pl.ds(at, BAND), :].reshape(boxes * BAND, TS)
                total = jnp.dot(
                    mix_hi[...].reshape(G * G * BAND, boxes * BAND),
                    tiles,
                    preferred_element_type=F32,
                )
                total = total + jnp.dot(
                    mix_lo[...].reshape(G * G * BAND, boxes * BAND),
                    tiles,
                    preferred_element_type=F32,
                )
                total = total.astype(BF16).reshape(G, G, BAND, TS)
                to = pl.multiple_of(i * BAND, BAND)
                for g in range(G):
                    sums[c, g * parts + h, :, pl.ds(to, BAND), :] = total[g]
                return 0

            lax.fori_loop(0, step_rows // BAND, band, 0)
        for d in range(1, n_visit):
            visit_copy(c, d).start()

    match(0)
    pl.semaphore_wait(barrier, n_patch - 1 + n_visit - 1 + len(corners))
    send_patch(0)

    lanes = lax.broadcasted_iota(jnp.int32, (BAND, boxes * BAND), 1)
    sublanes = lax.broadcasted_iota(jnp.int32, (BAND, boxes * BAND), 0)
    diagonal = lax.rem(lanes, BAND) == sublanes
    lane_box = lanes // BAND

    def gather(b, carry):
        slots, weights = carry
        start = (v * n_patch + b // CAP) * per_device
        entry, filled = entry_for(start, p, lax.rem(b, CAP))
        value = jnp.where(filled > 0, weight[(start + entry) // K_OV], 0.0)
        here = lane_box == b
        return (
            jnp.where(here, slot[start + entry], slots),
            jnp.where(here, value, weights),
        )

    slots, weights = lax.fori_loop(
        0,
        boxes,
        gather,
        (jnp.zeros(lanes.shape, jnp.int32), jnp.zeros(lanes.shape, F32)),
    )

    def mix(s, _):
        full = jnp.where(jnp.logical_and(slots == s, diagonal), weights, 0.0)
        high = full.astype(BF16)
        mix_hi[s] = high
        mix_lo[s] = (full - high.astype(F32)).astype(BF16)
        return 0

    lax.fori_loop(0, G * G, mix, 0)

    def step(c, _):
        match(c + 1)
        send_patch(c + 1)
        combine(c)
        return 0

    lax.fori_loop(0, STEPS - 1, step, 0)
    combine(STEPS - 1)

    tile_row = (v * rows) // TS
    scales = []
    for g in range(G):
        chosen = jnp.logical_and(target_v[...] == p, slot_v[...] == tile_row * G + g)
        scales.append(1.0 + jnp.sum(jnp.where(chosen, weight_v[...], 0.0)))

    def finish(c, _):
        for d in range(1, n_visit):
            visit_copy(c, d).wait_recv()
        for g in range(G):
            total = sums[c, v, g].astype(F32)
            for d in range(1, n_visit):
                total = total + arrived[c, d - 1, g].astype(F32)
            value = total / scales[g]
            at = pl.multiple_of(c * step_rows, step_rows)
            coadd[pl.ds(at, step_rows), g * TS : (g + 1) * TS] = value
            ext[pl.ds(EDGE_R + at, step_rows), EDGE_C + g * TS : EDGE_C + (g + 1) * TS] = value
        return 0

    lax.fori_loop(0, STEPS, finish, 0)

    def span(shift, edge, length):
        if shift < 0:
            return pl.ds(edge, edge), pl.ds(edge + length, edge)
        if shift > 0:
            return pl.ds(length, edge), pl.ds(0, edge)
        return pl.ds(edge, length), pl.ds(edge, length)

    def border(k, dv, dp):
        r_from, r_to = span(dv, EDGE_R, rows)
        c_from, c_to = span(dp, EDGE_C, width)
        return pltpu.make_async_remote_copy(
            src_ref=ext.at[r_from, c_from],
            dst_ref=ext.at[r_to, c_to],
            send_sem=h_send.at[k],
            recv_sem=h_recv.at[k],
            device_id=(v + dv, p + dp),
            device_id_type=MESH,
        )

    around = sides + corners
    for k, (dv, dp) in enumerate(around):

        @pl.when(inside(dv, dp))
        def _():
            border(k, dv, dp).start()

    for k, (dv, dp) in enumerate(around):

        @pl.when(inside(-dv, -dp))
        def _():
            border(k, dv, dp).wait_recv()

    count = taps.shape[0]
    radius = count // 2
    block = 16

    def filtered(i, _):
        at = pl.multiple_of(i * block, block)
        held = ext[pl.ds(at, block + 2 * EDGE_R), :]
        low = EDGE_R - radius
        across = taps[0] * held[low : low + block, :]
        for j in range(1, count):
            across = across + taps[j] * held[low + j : low + j + block, :]
        low = EDGE_C - radius
        result = taps[0] * across[:, low : low + width]
        for j in range(1, count):
            result = result + taps[j] * across[:, low + j : low + j + width]
        detection[pl.ds(at, block), :] = result
        return 0

    lax.fori_loop(0, rows // block, filtered, 0)

    for k, (dv, dp) in enumerate(around):

        @pl.when(inside(dv, dp))
        def _():
            border(k, dv, dp).wait_send()

    def drain(c, _):
        for d in range(1, n_patch):
            patch_copy(c, d).wait_send()
        for d in range(1, n_visit):
            visit_copy(c, d).wait_send()
        return 0

    lax.fori_loop(0, STEPS, drain, 0)


def body(
    ccd_images,
    ccd_weight,
    psf_index,
    patch_target,
    tile_slot,
    row_matrix,
    col_matrix,
    warp_rows,
    warp_cols,
    psf_match,
    detect_kernel,
):
    n_visit = lax.axis_size("visit")
    n_patch = lax.axis_size("patch")
    rows = G * TS // n_visit
    width = G * TS
    step_rows = rows // STEPS
    high = TS // rows * step_rows
    boxes = n_patch * CAP
    targets = patch_target[:, 0]
    entries = targets.shape[0]
    vector = (entries // 128, 128)
    smem = pl.BlockSpec(memory_space=pltpu.SMEM)
    vmem = pl.BlockSpec(memory_space=pltpu.VMEM)
    out = jax.ShapeDtypeStruct((rows, width), F32)
    return pl.pallas_call(
        functools.partial(kernel, n_visit, n_patch),
        out_shape=(out, out),
        in_specs=[vmem] * 4 + [smem] * 7 + [vmem] * 3,
        out_specs=(vmem, vmem),
        scratch_shapes=[
            pltpu.VMEM((boxes, TS, TS), BF16),
            pltpu.SMEM((boxes,), jnp.int32),
            pltpu.VMEM((STEPS, boxes, high, TS), BF16),
            pltpu.VMEM((STEPS, boxes, high, TS), BF16),
            pltpu.VMEM((STEPS, n_visit, G, step_rows, TS), BF16),
            pltpu.VMEM((STEPS, n_visit - 1, G, step_rows, TS), BF16),
            pltpu.VMEM((G * G, BAND, boxes * BAND), BF16),
            pltpu.VMEM((G * G, BAND, boxes * BAND), BF16),
            pltpu.VMEM((rows + 2 * EDGE_R, width + 2 * EDGE_C), F32),
            pltpu.SemaphoreType.DMA((STEPS, n_patch - 1)),
            pltpu.SemaphoreType.DMA((STEPS, n_patch - 1)),
            pltpu.SemaphoreType.DMA((STEPS, n_visit - 1)),
            pltpu.SemaphoreType.DMA((STEPS, n_visit - 1)),
            pltpu.SemaphoreType.DMA((8,)),
            pltpu.SemaphoreType.DMA((8,)),
        ],
        compiler_params=pltpu.CompilerParams(
            collective_id=0, has_side_effects=True, vmem_limit_bytes=48 * 1024 * 1024
        ),
    )(
        ccd_images,
        warp_rows,
        warp_cols,
        psf_match,
        detect_kernel,
        ccd_weight,
        psf_index,
        targets,
        tile_slot,
        row_matrix,
        col_matrix,
        targets.reshape(vector),
        tile_slot.reshape(vector),
        jnp.repeat(ccd_weight, K_OV).reshape(vector),
    )


def solution(mesh):
    in_specs = (P(("visit", "patch"), None, None), P(), P(), P(), P(), P(), P(), P(), P(), P(), P())
    out_specs = (P("visit", "patch"), P("visit", "patch"))
    return jax.shard_map(body, mesh=mesh, in_specs=in_specs, out_specs=out_specs, check_vma=False)
```

```python
import functools

import jax
import jax.numpy as jnp
from jax import lax
from jax.experimental import pallas as pl
from jax.experimental.pallas import tpu as pltpu
from jax.sharding import PartitionSpec as P

K_OV = 4
TS = 256
G = 4
CAP = 2
STEPS = 8
AHEAD = 2
BAND = 16
EDGE_R = 8
EDGE_C = 128
MESH = pl.DeviceIdType.MESH
F32 = jnp.float32
BF16 = jnp.bfloat16
NT = (((1,), (1,)), ((), ()))


def kernel(
    n_visit,
    n_patch,
    images_hbm,
    rows_hbm,
    cols_hbm,
    psf_hbm,
    taps,
    weight,
    psf_index,
    target,
    slot,
    row_pick,
    col_pick,
    coadd,
    detection,
    images,
    row_tables,
    col_tables,
    psf_tables,
    matched,
    entry_of,
    slot_weight,
    outbox,
    inbox,
    sums,
    arrived,
    mix,
    ext,
    load_sem,
    p_send,
    p_recv,
    v_send,
    v_recv,
    c_send,
    c_recv,
    r_send,
    r_recv,
):
    v = lax.axis_index("visit")
    p = lax.axis_index("patch")
    n_images = images.shape[0]
    per_device = n_images * K_OV
    boxes = n_patch * CAP
    rows = coadd.shape[0]
    width = coadd.shape[1]
    step_rows = rows // STEPS
    parts = TS // rows
    own = v * n_patch + p
    base = own * per_device

    loads = [
        pltpu.make_async_copy(rows_hbm, row_tables, load_sem.at[0]),
        pltpu.make_async_copy(images_hbm, images, load_sem.at[1]),
        pltpu.make_async_copy(cols_hbm, col_tables, load_sem.at[2]),
        pltpu.make_async_copy(psf_hbm, psf_tables, load_sem.at[3]),
    ]
    for load in loads:
        load.start()

    def entry_for(start, patch, rank):
        seen = jnp.int32(0)
        found = jnp.int32(0)
        filled = jnp.int32(0)
        for e in range(per_device):
            hit = target[start + e] == patch
            take = jnp.logical_and(hit, seen == rank)
            found = jnp.where(take, e, found)
            filled = jnp.where(take, 1, filled)
            seen = seen + hit.astype(jnp.int32)
        return found, filled

    ext[...] = jnp.zeros_like(ext)
    arrived[0, :, 0] = jnp.zeros_like(arrived[0, :, 0])
    arrived[1, :, n_visit - 1] = jnp.zeros_like(arrived[1, :, n_visit - 1])
    corners = [(-1, -1), (-1, 1), (1, -1), (1, 1)]
    barrier = pltpu.get_barrier_semaphore()
    for d in range(1, n_patch):
        pl.semaphore_signal(
            barrier, inc=1, device_id=(v, lax.rem(p + d, n_patch)), device_id_type=MESH
        )
    for d in (1, n_visit - 1):
        pl.semaphore_signal(
            barrier, inc=1, device_id=(lax.rem(v + d, n_visit), p), device_id_type=MESH
        )
    for dv, dp in corners:
        there = (lax.rem(v + dv + n_visit, n_visit), lax.rem(p + dp + n_patch, n_patch))
        pl.semaphore_signal(barrier, inc=1, device_id=there, device_id_type=MESH)

    def inside(dv, dp):
        ok = None
        for at, shift, count in ((v, dv, n_visit), (p, dp, n_patch)):
            if shift < 0:
                term = at > 0
            elif shift > 0:
                term = at < count - 1
            else:
                continue
            ok = term if ok is None else jnp.logical_and(ok, term)
        return ok

    def find(s, _):
        entry_of[s] = entry_for(base, s // CAP, lax.rem(s, CAP))[0]
        return 0

    lax.fori_loop(0, boxes, find, 0)
    for load in loads:
        load.wait()

    def warp(i, _):
        image = images[i]
        table = psf_tables[psf_index[own * n_images + i]]
        at = base + i * K_OV
        first = [
            jnp.dot(row_tables[row_pick[at + j]], image, preferred_element_type=F32).astype(BF16)
            for j in range(K_OV)
        ]
        second = [
            lax.dot_general(
                first[j], col_tables[col_pick[at + j]], NT, preferred_element_type=F32
            ).astype(BF16)
            for j in range(K_OV)
        ]
        third = [
            jnp.dot(table, second[j], preferred_element_type=F32).astype(BF16)
            for j in range(K_OV)
        ]
        for j in range(K_OV):
            matched[i * K_OV + j] = lax.dot_general(
                third[j], table, NT, preferred_element_type=F32
            ).astype(BF16)
        return 0

    lax.fori_loop(0, n_images, warp, 0)

    def patch_copy(c, d):
        there = lax.rem(p + d, n_patch)
        return pltpu.make_async_remote_copy(
            src_ref=outbox.at[c, pl.ds(there * CAP, CAP)],
            dst_ref=inbox.at[c, pl.ds(p * CAP, CAP)],
            send_sem=p_send.at[c, d - 1],
            recv_sem=p_recv.at[c, d - 1],
            device_id=(v, there),
            device_id_type=MESH,
        )

    def send_patch(c):
        def fill(s, _):
            for h in range(parts):
                at = pl.multiple_of(h * rows + c * step_rows, step_rows)
                outbox[c, s, h * step_rows : (h + 1) * step_rows, :] = matched[
                    entry_of[s], pl.ds(at, step_rows), :
                ]
            return 0

        lax.fori_loop(0, boxes, fill, 0)
        for d in range(1, n_patch):
            patch_copy(c, d).start()
        inbox[c, pl.ds(p * CAP, CAP)] = outbox[c, pl.ds(p * CAP, CAP)]

    def hop(c, r, up):
        way = 0 if up else 1
        return pltpu.make_async_remote_copy(
            src_ref=sums.at[c, r],
            dst_ref=arrived.at[way, c, r],
            send_sem=v_send.at[way, c, r],
            recv_sem=v_recv.at[way, c, r],
            device_id=(v + (1 if up else -1), p),
            device_id_type=MESH,
        )

    def pass_on(c, up, add):
        for r in reversed(range(1, n_visit)) if up else range(n_visit - 1):

            @pl.when(v < r if up else v > r)
            def _():
                if add:
                    hop(c, r, up).wait_recv()
                    came = arrived[0 if up else 1, c, r].astype(F32)
                    sums[c, r] = (sums[c, r].astype(F32) + came).astype(BF16)
                hop(c, r, up).start()

    def combine(c):
        for d in range(1, n_patch):
            patch_copy(c, d).wait_recv()
        weights = mix[...].reshape(G * G * BAND, boxes * BAND)
        for h in range(parts):
            for i in range(step_rows // BAND):
                at = h * step_rows + i * BAND
                tiles = inbox[c, :, at : at + BAND, :].reshape(boxes * BAND, TS)
                total = jnp.dot(weights, tiles, preferred_element_type=F32)
                total = total.astype(BF16).reshape(G, G, BAND, TS)
                for g in range(G):
                    sums[c, g * parts + h, :, i * BAND : (i + 1) * BAND, :] = total[g]

        @pl.when(v == 0)
        def _():
            pass_on(c, True, False)

        @pl.when(v == n_visit - 1)
        def _():
            pass_on(c, False, False)

    def forward(c):
        @pl.when(jnp.logical_and(v > 0, 2 * v < n_visit))
        def _():
            pass_on(c, True, True)
            pass_on(c, False, True)

        @pl.when(jnp.logical_and(v < n_visit - 1, 2 * v >= n_visit))
        def _():
            pass_on(c, False, True)
            pass_on(c, True, True)

    def column_copy(c, k):
        at = pl.multiple_of(EDGE_R + c * step_rows, 8)
        here, there = (EDGE_C, EDGE_C + width) if k == 0 else (width, 0)
        return pltpu.make_async_remote_copy(
            src_ref=ext.at[pl.ds(at, step_rows), pl.ds(here, EDGE_C)],
            dst_ref=ext.at[pl.ds(at, step_rows), pl.ds(there, EDGE_C)],
            send_sem=c_send.at[k, c],
            recv_sem=c_recv.at[k, c],
            device_id=(v, p + (-1 if k == 0 else 1)),
            device_id_type=MESH,
        )

    def span(shift, edge, length):
        if shift < 0:
            return pl.ds(edge, edge), pl.ds(edge + length, edge)
        if shift > 0:
            return pl.ds(length, edge), pl.ds(0, edge)
        return pl.ds(edge, length), pl.ds(edge, length)

    around = [(-1, 0), (1, 0)] + corners

    def row_copy(k):
        dv, dp = around[k]
        r_from, r_to = span(dv, EDGE_R, rows)
        c_from, c_to = span(dp, EDGE_C, width)
        return pltpu.make_async_remote_copy(
            src_ref=ext.at[r_from, c_from],
            dst_ref=ext.at[r_to, c_to],
            send_sem=r_send.at[k],
            recv_sem=r_recv.at[k],
            device_id=(v + dv, p + dp),
            device_id_type=MESH,
        )

    def finish(c):
        @pl.when(v > 0)
        def _():
            hop(c, v, True).wait_recv()

        @pl.when(v < n_visit - 1)
        def _():
            hop(c, v, False).wait_recv()

        at = pl.multiple_of(c * step_rows, step_rows)
        for g in range(G):
            total = sums[c, v, g].astype(F32)
            total = total + arrived[0, c, v, g].astype(F32)
            total = total + arrived[1, c, v, g].astype(F32)
            value = total * (1.0 / (1.0 + jnp.full((1, TS), slot_weight[g])))
            coadd[pl.ds(at, step_rows), g * TS : (g + 1) * TS] = value
            ext[pl.ds(EDGE_R + at, step_rows), EDGE_C + g * TS : EDGE_C + (g + 1) * TS] = value
        for k in range(2):

            @pl.when(inside(0, -1 if k == 0 else 1))
            def _():
                column_copy(c, k).start()

        for k, (dv, dp) in enumerate(around):

            @pl.when(jnp.logical_and(c == (0 if dv < 0 else STEPS - 1), inside(dv, dp)))
            def _():
                row_copy(k).start()

    def columns_in(c):
        for k in range(2):

            @pl.when(inside(0, 1 if k == 0 else -1))
            def _():
                column_copy(c, k).wait_recv()

    count = taps.shape[0]
    radius = count // 2

    def detect(c):
        def one(i, _):
            at = pl.multiple_of(c * step_rows + i * BAND, BAND)
            held = ext[pl.ds(at, BAND + 2 * EDGE_R), :]
            low = EDGE_R - radius
            across = taps[0] * held[low : low + BAND, :]
            for j in range(1, count):
                across = across + taps[j] * held[low + j : low + j + BAND, :]
            low = EDGE_C - radius
            result = taps[0] * across[:, low : low + width]
            for j in range(1, count):
                result = result + taps[j] * across[:, low + j : low + j + width]
            detection[pl.ds(at, BAND), :] = result
            return 0

        lax.fori_loop(0, step_rows // BAND, one, 0)

    pl.semaphore_wait(barrier, n_patch - 1 + 2 + len(corners))
    for c in range(AHEAD):
        send_patch(c)

    lanes = lax.broadcasted_iota(jnp.int32, (BAND, boxes * BAND), 1)
    sublanes = lax.broadcasted_iota(jnp.int32, (BAND, boxes * BAND), 0)
    diagonal = lax.rem(lanes, BAND) == sublanes
    lane_box = lanes // BAND

    def gather(b, carry):
        slots, weights = carry
        start = (v * n_patch + b // CAP) * per_device
        entry, filled = entry_for(start, p, lax.rem(b, CAP))
        value = jnp.where(filled > 0, weight[(start + entry) // K_OV], 0.0)
        here = lane_box == b
        return (
            jnp.where(here, slot[start + entry], slots),
            jnp.where(here, value, weights),
        )

    slots, weights = lax.fori_loop(
        0,
        boxes,
        gather,
        (jnp.zeros(lanes.shape, jnp.int32), jnp.zeros(lanes.shape, F32)),
    )

    def place(s, _):
        full = jnp.where(jnp.logical_and(slots == s, diagonal), weights, 0.0)
        mix[s] = full.astype(BF16)
        return 0

    lax.fori_loop(0, G * G, place, 0)

    tile_row = (v * rows) // TS

    def tally(i, carry):
        carry = list(carry)
        for j in range(K_OV):
            e = i * K_OV + j
            mine = target[e] == p
            at = slot[e] - tile_row * G
            for g in range(G):
                chosen = jnp.logical_and(mine, at == g)
                carry[g] = carry[g] + jnp.where(chosen, weight[i], 0.0)
        return tuple(carry)

    totals = lax.fori_loop(0, weight.shape[0], tally, (jnp.float32(0),) * G)
    for g in range(G):
        slot_weight[g] = totals[g]

    def stage(t, first, last, do):
        @pl.when(jnp.logical_and(t >= first, t <= last))
        def _():
            do()

    def step(t, _):
        stage(t, 0, STEPS - 1 - AHEAD, lambda: send_patch(t + AHEAD))
        stage(t, 0, STEPS - 1, lambda: combine(t))
        stage(t, 1, STEPS, lambda: forward(t - 1))
        stage(t, 2, STEPS + 1, lambda: finish(t - 2))
        stage(t, 3, STEPS + 2, lambda: columns_in(t - 3))
        stage(t, 5, STEPS + 2, lambda: detect(t - 4))
        return 0

    lax.fori_loop(0, STEPS + 3, step, 0)
    for k, (dv, dp) in enumerate(around):

        @pl.when(inside(-dv, -dp))
        def _():
            row_copy(k).wait_recv()

    detect(STEPS - 1)
    detect(0)

    for k, (dv, dp) in enumerate(around):

        @pl.when(inside(dv, dp))
        def _():
            row_copy(k).wait_send()

    def drain(c, _):
        for d in range(1, n_patch):
            patch_copy(c, d).wait_send()
        for k in range(2):

            @pl.when(inside(0, -1 if k == 0 else 1))
            def _():
                column_copy(c, k).wait_send()

        for r in range(n_visit):

            @pl.when(jnp.logical_and(v < r, v < n_visit - 1))
            def _():
                hop(c, r, True).wait_send()

            @pl.when(jnp.logical_and(v > r, v > 0))
            def _():
                hop(c, r, False).wait_send()

        return 0

    lax.fori_loop(0, STEPS, drain, 0)


def body(
    ccd_images,
    ccd_weight,
    psf_index,
    patch_target,
    tile_slot,
    row_matrix,
    col_matrix,
    warp_rows,
    warp_cols,
    psf_match,
    detect_kernel,
):
    n_visit = lax.axis_size("visit")
    n_patch = lax.axis_size("patch")
    rows = G * TS // n_visit
    width = G * TS
    step_rows = rows // STEPS
    high = TS // rows * step_rows
    boxes = n_patch * CAP
    smem = pl.BlockSpec(memory_space=pltpu.SMEM)
    vmem = pl.BlockSpec(memory_space=pltpu.VMEM)
    hbm = pl.BlockSpec(memory_space=pl.ANY)
    out = jax.ShapeDtypeStruct((rows, width), F32)
    return pl.pallas_call(
        functools.partial(kernel, n_visit, n_patch),
        out_shape=(out, out),
        in_specs=[hbm] * 4 + [smem] * 7,
        out_specs=(vmem, vmem),
        scratch_shapes=[
            pltpu.VMEM(ccd_images.shape, BF16),
            pltpu.VMEM(warp_rows.shape, BF16),
            pltpu.VMEM(warp_cols.shape, BF16),
            pltpu.VMEM(psf_match.shape, BF16),
            pltpu.VMEM((ccd_images.shape[0] * K_OV, TS, TS), BF16),
            pltpu.SMEM((boxes,), jnp.int32),
            pltpu.SMEM((G,), F32),
            pltpu.VMEM((STEPS, boxes, high, TS), BF16),
            pltpu.VMEM((STEPS, boxes, high, TS), BF16),
            pltpu.VMEM((STEPS, n_visit, G, step_rows, TS), BF16),
            pltpu.VMEM((2, STEPS, n_visit, G, step_rows, TS), BF16),
            pltpu.VMEM((G * G, BAND, boxes * BAND), BF16),
            pltpu.VMEM((rows + 2 * EDGE_R, width + 2 * EDGE_C), F32),
            pltpu.SemaphoreType.DMA((4,)),
            pltpu.SemaphoreType.DMA((STEPS, n_patch - 1)),
            pltpu.SemaphoreType.DMA((STEPS, n_patch - 1)),
            pltpu.SemaphoreType.DMA((2, STEPS, n_visit)),
            pltpu.SemaphoreType.DMA((2, STEPS, n_visit)),
            pltpu.SemaphoreType.DMA((2, STEPS)),
            pltpu.SemaphoreType.DMA((2, STEPS)),
            pltpu.SemaphoreType.DMA((6,)),
            pltpu.SemaphoreType.DMA((6,)),
        ],
        compiler_params=pltpu.CompilerParams(
            collective_id=0, has_side_effects=True, vmem_limit_bytes=56 * 1024 * 1024
        ),
    )(
        ccd_images,
        warp_rows,
        warp_cols,
        psf_match,
        detect_kernel,
        ccd_weight,
        psf_index,
        patch_target[:, 0],
        tile_slot,
        row_matrix,
        col_matrix,
    )


def solution(mesh):
    in_specs = (P(("visit", "patch"), None, None), P(), P(), P(), P(), P(), P(), P(), P(), P(), P())
    out_specs = (P("visit", "patch"), P("visit", "patch"))
    return jax.shard_map(body, mesh=mesh, in_specs=in_specs, out_specs=out_specs, check_vma=False)
```

```python
import functools

import jax
import jax.numpy as jnp
from jax import lax
from jax.experimental import pallas as pl
from jax.experimental.pallas import tpu as pltpu
from jax.sharding import PartitionSpec as P

K_OV = 4
TS = 256
G = 4
CAP = 2
STEPS = 8
AHEAD = 2
LAG = 4
BAND = 16
EDGE_R = 8
EDGE_C = 128
MESH = pl.DeviceIdType.MESH
F32 = jnp.float32
BF16 = jnp.bfloat16
NT = (((1,), (1,)), ((), ()))


def kernel(
    n_visit,
    n_patch,
    images_hbm,
    rows_hbm,
    cols_hbm,
    psf_hbm,
    taps,
    weight,
    psf_index,
    target,
    slot,
    row_pick,
    col_pick,
    out,
    images,
    row_tables,
    col_tables,
    psf_tables,
    matched,
    entry_of,
    slot_weight,
    outbox,
    inbox,
    sums,
    arrived,
    mix,
    ext,
    filtered,
    load_sem,
    o_sem,
    p_send,
    p_recv,
    v_send,
    v_recv,
    c_send,
    c_recv,
    r_send,
    r_recv,
):
    v = lax.axis_index("visit")
    p = lax.axis_index("patch")
    n_images = images.shape[0]
    per_device = n_images * K_OV
    boxes = n_patch * CAP
    rows = out.shape[1]
    width = out.shape[2]
    step_rows = rows // STEPS
    parts = TS // rows
    own = v * n_patch + p
    base = own * per_device

    loads = [
        pltpu.make_async_copy(rows_hbm, row_tables, load_sem.at[0]),
        pltpu.make_async_copy(images_hbm, images, load_sem.at[1]),
        pltpu.make_async_copy(cols_hbm, col_tables, load_sem.at[2]),
        pltpu.make_async_copy(psf_hbm, psf_tables, load_sem.at[3]),
    ]
    for load in loads:
        load.start()

    def entry_for(start, patch, rank):
        seen = jnp.int32(0)
        found = jnp.int32(0)
        filled = jnp.int32(0)
        for e in range(per_device):
            hit = target[start + e] == patch
            take = jnp.logical_and(hit, seen == rank)
            found = jnp.where(take, e, found)
            filled = jnp.where(take, 1, filled)
            seen = seen + hit.astype(jnp.int32)
        return found, filled

    ext[...] = jnp.zeros_like(ext)
    arrived[0, :, 0] = jnp.zeros_like(arrived[0, :, 0])
    arrived[1, :, n_visit - 1] = jnp.zeros_like(arrived[1, :, n_visit - 1])
    corners = [(-1, -1), (-1, 1), (1, -1), (1, 1)]
    barrier = pltpu.get_barrier_semaphore()
    for d in range(1, n_patch):
        pl.semaphore_signal(
            barrier, inc=1, device_id=(v, lax.rem(p + d, n_patch)), device_id_type=MESH
        )
    for d in (1, n_visit - 1):
        pl.semaphore_signal(
            barrier, inc=1, device_id=(lax.rem(v + d, n_visit), p), device_id_type=MESH
        )
    for dv, dp in corners:
        there = (lax.rem(v + dv + n_visit, n_visit), lax.rem(p + dp + n_patch, n_patch))
        pl.semaphore_signal(barrier, inc=1, device_id=there, device_id_type=MESH)

    def inside(dv, dp):
        ok = None
        for at, shift, count in ((v, dv, n_visit), (p, dp, n_patch)):
            if shift < 0:
                term = at > 0
            elif shift > 0:
                term = at < count - 1
            else:
                continue
            ok = term if ok is None else jnp.logical_and(ok, term)
        return ok

    def find(s, _):
        entry_of[s] = entry_for(base, s // CAP, lax.rem(s, CAP))[0]
        return 0

    lax.fori_loop(0, boxes, find, 0)
    for load in loads:
        load.wait()

    def warp(i, _):
        image = images[i]
        table = psf_tables[psf_index[own * n_images + i]]
        at = base + i * K_OV
        first = [
            jnp.dot(row_tables[row_pick[at + j]], image, preferred_element_type=F32).astype(BF16)
            for j in range(K_OV)
        ]
        second = [
            lax.dot_general(
                first[j], col_tables[col_pick[at + j]], NT, preferred_element_type=F32
            ).astype(BF16)
            for j in range(K_OV)
        ]
        third = [
            jnp.dot(table, second[j], preferred_element_type=F32).astype(BF16)
            for j in range(K_OV)
        ]
        for j in range(K_OV):
            matched[i * K_OV + j] = lax.dot_general(
                third[j], table, NT, preferred_element_type=F32
            ).astype(BF16)
        return 0

    lax.fori_loop(0, n_images, warp, 0)

    def patch_copy(c, d):
        there = lax.rem(p + d, n_patch)
        return pltpu.make_async_remote_copy(
            src_ref=outbox.at[c, pl.ds(there * CAP, CAP)],
            dst_ref=inbox.at[c, pl.ds(p * CAP, CAP)],
            send_sem=p_send.at[c, d - 1],
            recv_sem=p_recv.at[c, d - 1],
            device_id=(v, there),
            device_id_type=MESH,
        )

    def send_patch(c):
        def fill(s, _):
            for h in range(parts):
                at = pl.multiple_of(h * rows + c * step_rows, step_rows)
                outbox[c, s, h * step_rows : (h + 1) * step_rows, :] = matched[
                    entry_of[s], pl.ds(at, step_rows), :
                ]
            return 0

        lax.fori_loop(0, boxes, fill, 0)
        for d in range(1, n_patch):
            patch_copy(c, d).start()
        inbox[c, pl.ds(p * CAP, CAP)] = outbox[c, pl.ds(p * CAP, CAP)]

    def hop(c, r, up):
        way = 0 if up else 1
        return pltpu.make_async_remote_copy(
            src_ref=sums.at[c, r],
            dst_ref=arrived.at[way, c, r],
            send_sem=v_send.at[way, c, r],
            recv_sem=v_recv.at[way, c, r],
            device_id=(v + (1 if up else -1), p),
            device_id_type=MESH,
        )

    def pass_on(c, up, add):
        for r in reversed(range(1, n_visit)) if up else range(n_visit - 1):

            @pl.when(v < r if up else v > r)
            def _():
                if add:
                    hop(c, r, up).wait_recv()
                    came = arrived[0 if up else 1, c, r].astype(F32)
                    sums[c, r] = (sums[c, r].astype(F32) + came).astype(BF16)
                hop(c, r, up).start()

    def combine(c):
        for d in range(1, n_patch):
            patch_copy(c, d).wait_recv()
        weights = mix[...].reshape(G * G * BAND, boxes * BAND)
        for h in range(parts):
            for i in range(step_rows // BAND):
                at = h * step_rows + i * BAND
                tiles = inbox[c, :, at : at + BAND, :].reshape(boxes * BAND, TS)
                total = jnp.dot(weights, tiles, preferred_element_type=F32)
                total = total.astype(BF16).reshape(G, G, BAND, TS)
                for g in range(G):
                    sums[c, g * parts + h, :, i * BAND : (i + 1) * BAND, :] = total[g]

        @pl.when(v == 0)
        def _():
            pass_on(c, True, False)

        @pl.when(v == n_visit - 1)
        def _():
            pass_on(c, False, False)

    def forward(c, near):
        low = 2 * v < n_visit

        @pl.when(jnp.logical_and(v > 0, low if near else jnp.logical_not(low)))
        def _():
            pass_on(c, True, True)

        @pl.when(jnp.logical_and(v < n_visit - 1, jnp.logical_not(low) if near else low))
        def _():
            pass_on(c, False, True)

    def column_copy(c, k):
        at = pl.multiple_of(EDGE_R + c * step_rows, 8)
        here, there = (EDGE_C, EDGE_C + width) if k == 0 else (width, 0)
        return pltpu.make_async_remote_copy(
            src_ref=ext.at[pl.ds(at, step_rows), pl.ds(here, EDGE_C)],
            dst_ref=ext.at[pl.ds(at, step_rows), pl.ds(there, EDGE_C)],
            send_sem=c_send.at[k, c],
            recv_sem=c_recv.at[k, c],
            device_id=(v, p + (-1 if k == 0 else 1)),
            device_id_type=MESH,
        )

    def span(shift, edge, length):
        if shift < 0:
            return pl.ds(edge, edge), pl.ds(edge + length, edge)
        if shift > 0:
            return pl.ds(length, edge), pl.ds(0, edge)
        return pl.ds(edge, length), pl.ds(edge, length)

    around = [(-1, 0), (1, 0)] + corners

    def row_copy(k):
        dv, dp = around[k]
        r_from, r_to = span(dv, EDGE_R, rows)
        c_from, c_to = span(dp, EDGE_C, width)
        return pltpu.make_async_remote_copy(
            src_ref=ext.at[r_from, c_from],
            dst_ref=ext.at[r_to, c_to],
            send_sem=r_send.at[k],
            recv_sem=r_recv.at[k],
            device_id=(v + dv, p + dp),
            device_id_type=MESH,
        )

    def store(c, k):
        at = pl.multiple_of(c * step_rows, step_rows)
        if k == 0:
            here = ext.at[pl.ds(pl.multiple_of(EDGE_R + at, 8), step_rows), pl.ds(EDGE_C, width)]
        else:
            here = filtered.at[pl.ds(at, step_rows)]
        return pltpu.make_async_copy(here, out.at[k, pl.ds(at, step_rows)], o_sem.at[k, c])

    def finish(c):
        @pl.when(v > 0)
        def _():
            hop(c, v, True).wait_recv()

        @pl.when(v < n_visit - 1)
        def _():
            hop(c, v, False).wait_recv()

        at = pl.multiple_of(c * step_rows, step_rows)
        for g in range(G):
            total = sums[c, v, g].astype(F32)
            total = total + arrived[0, c, v, g].astype(F32)
            total = total + arrived[1, c, v, g].astype(F32)
            value = total * (1.0 / (1.0 + jnp.full((1, TS), slot_weight[g])))
            ext[pl.ds(EDGE_R + at, step_rows), EDGE_C + g * TS : EDGE_C + (g + 1) * TS] = value
        store(c, 0).start()
        for k in range(2):

            @pl.when(inside(0, -1 if k == 0 else 1))
            def _():
                column_copy(c, k).start()

        for k, (dv, dp) in enumerate(around):

            @pl.when(jnp.logical_and(c == (0 if dv < 0 else STEPS - 1), inside(dv, dp)))
            def _():
                row_copy(k).start()

    def columns_in(c):
        for k in range(2):

            @pl.when(inside(0, 1 if k == 0 else -1))
            def _():
                column_copy(c, k).wait_recv()

    count = taps.shape[0]
    radius = count // 2

    def detect(c):
        def one(i, _):
            at = pl.multiple_of(c * step_rows + i * BAND, BAND)
            held = ext[pl.ds(at, BAND + 2 * EDGE_R), :]
            low = EDGE_R - radius
            across = taps[0] * held[low : low + BAND, :]
            for j in range(1, count):
                across = across + taps[j] * held[low + j : low + j + BAND, :]
            low = EDGE_C - radius
            result = taps[0] * across[:, low : low + width]
            for j in range(1, count):
                result = result + taps[j] * across[:, low + j : low + j + width]
            filtered[pl.ds(at, BAND), :] = result
            return 0

        lax.fori_loop(0, step_rows // BAND, one, 0)
        store(c, 1).start()

    pl.semaphore_wait(barrier, n_patch - 1 + 2 + len(corners))
    for c in range(AHEAD):
        send_patch(c)

    lanes = lax.broadcasted_iota(jnp.int32, (BAND, boxes * BAND), 1)
    sublanes = lax.broadcasted_iota(jnp.int32, (BAND, boxes * BAND), 0)
    diagonal = lax.rem(lanes, BAND) == sublanes
    lane_box = lanes // BAND

    def gather(b, carry):
        slots, weights = carry
        start = (v * n_patch + b // CAP) * per_device
        entry, filled = entry_for(start, p, lax.rem(b, CAP))
        value = jnp.where(filled > 0, weight[(start + entry) // K_OV], 0.0)
        here = lane_box == b
        return (
            jnp.where(here, slot[start + entry], slots),
            jnp.where(here, value, weights),
        )

    slots, weights = lax.fori_loop(
        0,
        boxes,
        gather,
        (jnp.zeros(lanes.shape, jnp.int32), jnp.zeros(lanes.shape, F32)),
    )

    def place(s, _):
        full = jnp.where(jnp.logical_and(slots == s, diagonal), weights, 0.0)
        mix[s] = full.astype(BF16)
        return 0

    lax.fori_loop(0, G * G, place, 0)

    tile_row = (v * rows) // TS

    def tally(i, carry):
        carry = list(carry)
        for j in range(K_OV):
            e = i * K_OV + j
            at = jnp.where(target[e] == p, slot[e] - tile_row * G, -1)
            for g in range(G):
                carry[g] = carry[g] + jnp.where(at == g, weight[i], 0.0)
        return tuple(carry)

    def count_weights(k):
        half = weight.shape[0] // 2
        totals = tuple(jnp.float32(0) if k == 0 else slot_weight[g] for g in range(G))
        totals = lax.fori_loop(k * half, (k + 1) * half, tally, totals)
        for g in range(G):
            slot_weight[g] = totals[g]

    def stage(t, first, last, do):
        @pl.when(jnp.logical_and(t >= first, t <= last))
        def _():
            do()

    def step(t, _):
        stage(t, 0, STEPS - 1 - AHEAD, lambda: send_patch(t + AHEAD))
        stage(t, 0, STEPS - 1, lambda: combine(t))
        stage(t, 1, STEPS, lambda: forward(t - 1, True))
        stage(t, 2, STEPS + 1, lambda: forward(t - 2, False))
        stage(t, 2, 2, lambda: count_weights(0))
        stage(t, 3, 3, lambda: count_weights(1))
        stage(t, LAG, STEPS + LAG - 1, lambda: finish(t - LAG))
        stage(t, LAG + 1, STEPS + LAG, lambda: columns_in(t - LAG - 1))
        stage(t, LAG + 3, STEPS + LAG, lambda: detect(t - LAG - 2))
        return 0

    lax.fori_loop(0, STEPS + LAG + 1, step, 0)
    for k, (dv, dp) in enumerate(around):

        @pl.when(inside(-dv, -dp))
        def _():
            row_copy(k).wait_recv()

    detect(STEPS - 1)
    detect(0)

    for k, (dv, dp) in enumerate(around):

        @pl.when(inside(dv, dp))
        def _():
            row_copy(k).wait_send()

    def drain(c, _):
        for d in range(1, n_patch):
            patch_copy(c, d).wait_send()
        for k in range(2):
            store(c, k).wait()
        for k in range(2):

            @pl.when(inside(0, -1 if k == 0 else 1))
            def _():
                column_copy(c, k).wait_send()

        for r in range(n_visit):

            @pl.when(jnp.logical_and(v < r, v < n_visit - 1))
            def _():
                hop(c, r, True).wait_send()

            @pl.when(jnp.logical_and(v > r, v > 0))
            def _():
                hop(c, r, False).wait_send()

        return 0

    lax.fori_loop(0, STEPS, drain, 0)


def body(
    ccd_images,
    ccd_weight,
    psf_index,
    patch_target,
    tile_slot,
    row_matrix,
    col_matrix,
    warp_rows,
    warp_cols,
    psf_match,
    detect_kernel,
):
    n_visit = lax.axis_size("visit")
    n_patch = lax.axis_size("patch")
    rows = G * TS // n_visit
    width = G * TS
    step_rows = rows // STEPS
    high = TS // rows * step_rows
    boxes = n_patch * CAP
    smem = pl.BlockSpec(memory_space=pltpu.SMEM)
    hbm = pl.BlockSpec(memory_space=pl.ANY)
    out = jax.ShapeDtypeStruct((2, rows, width), F32)
    both = pl.pallas_call(
        functools.partial(kernel, n_visit, n_patch),
        out_shape=out,
        in_specs=[hbm] * 4 + [smem] * 7,
        out_specs=hbm,
        scratch_shapes=[
            pltpu.VMEM(ccd_images.shape, BF16),
            pltpu.VMEM(warp_rows.shape, BF16),
            pltpu.VMEM(warp_cols.shape, BF16),
            pltpu.VMEM(psf_match.shape, BF16),
            pltpu.VMEM((ccd_images.shape[0] * K_OV, TS, TS), BF16),
            pltpu.SMEM((boxes,), jnp.int32),
            pltpu.SMEM((G,), F32),
            pltpu.VMEM((STEPS, boxes, high, TS), BF16),
            pltpu.VMEM((STEPS, boxes, high, TS), BF16),
            pltpu.VMEM((STEPS, n_visit, G, step_rows, TS), BF16),
            pltpu.VMEM((2, STEPS, n_visit, G, step_rows, TS), BF16),
            pltpu.VMEM((G * G, BAND, boxes * BAND), BF16),
            pltpu.VMEM((rows + 2 * EDGE_R, width + 2 * EDGE_C), F32),
            pltpu.VMEM((rows, width), F32),
            pltpu.SemaphoreType.DMA((4,)),
            pltpu.SemaphoreType.DMA((2, STEPS)),
            pltpu.SemaphoreType.DMA((STEPS, n_patch - 1)),
            pltpu.SemaphoreType.DMA((STEPS, n_patch - 1)),
            pltpu.SemaphoreType.DMA((2, STEPS, n_visit)),
            pltpu.SemaphoreType.DMA((2, STEPS, n_visit)),
            pltpu.SemaphoreType.DMA((2, STEPS)),
            pltpu.SemaphoreType.DMA((2, STEPS)),
            pltpu.SemaphoreType.DMA((6,)),
            pltpu.SemaphoreType.DMA((6,)),
        ],
        compiler_params=pltpu.CompilerParams(
            collective_id=0, has_side_effects=True, vmem_limit_bytes=56 * 1024 * 1024
        ),
    )(
        ccd_images,
        warp_rows,
        warp_cols,
        psf_match,
        detect_kernel,
        ccd_weight,
        psf_index,
        patch_target[:, 0],
        tile_slot,
        row_matrix,
        col_matrix,
    )
    return both[0], both[1]


def solution(mesh):
    in_specs = (P(("visit", "patch"), None, None), P(), P(), P(), P(), P(), P(), P(), P(), P(), P())
    out_specs = (P("visit", "patch"), P("visit", "patch"))
    return jax.shard_map(body, mesh=mesh, in_specs=in_specs, out_specs=out_specs, check_vma=False)
```

```python
import functools

import jax
import jax.numpy as jnp
from jax import lax
from jax.experimental import pallas as pl
from jax.experimental.pallas import tpu as pltpu
from jax.sharding import PartitionSpec as P

K_OV = 4
TS = 256
G = 4
CAP = 2
STEPS = 8
AHEAD = 4
LAG = 6
BAND = 16
EDGE_R = 8
EDGE_C = 128
MESH = pl.DeviceIdType.MESH
F32 = jnp.float32
BF16 = jnp.bfloat16
NT = (((1,), (1,)), ((), ()))


def kernel(
    n_visit,
    n_patch,
    images_hbm,
    rows_hbm,
    cols_hbm,
    psf_hbm,
    taps,
    weight_hbm,
    psf_index_hbm,
    target_hbm,
    slot_hbm,
    row_pick_hbm,
    col_pick_hbm,
    coadd,
    detection,
    weight,
    psf_index,
    target,
    slot,
    row_pick,
    col_pick,
    images,
    row_tables,
    col_tables,
    psf_tables,
    matched,
    entry_of,
    slot_weight,
    outbox,
    inbox,
    sums,
    arrived,
    mix,
    ext,
    filtered,
    load_sem,
    o_sem,
    p_send,
    p_recv,
    v_send,
    v_recv,
    c_send,
    c_recv,
    r_send,
    r_recv,
):
    v = lax.axis_index("visit")
    p = lax.axis_index("patch")
    n_images = images.shape[0]
    per_device = n_images * K_OV
    boxes = n_patch * CAP
    rows = coadd.shape[0]
    width = coadd.shape[1]
    step_rows = rows // STEPS
    parts = TS // rows
    own = v * n_patch + p
    base = own * per_device

    lists = [
        pltpu.make_async_copy(target_hbm, target, load_sem.at[4]),
        pltpu.make_async_copy(slot_hbm, slot, load_sem.at[5]),
        pltpu.make_async_copy(row_pick_hbm, row_pick, load_sem.at[6]),
        pltpu.make_async_copy(col_pick_hbm, col_pick, load_sem.at[7]),
        pltpu.make_async_copy(psf_index_hbm, psf_index, load_sem.at[8]),
        pltpu.make_async_copy(weight_hbm, weight, load_sem.at[9]),
    ]
    loads = [
        pltpu.make_async_copy(rows_hbm, row_tables, load_sem.at[0]),
        pltpu.make_async_copy(images_hbm, images, load_sem.at[1]),
        pltpu.make_async_copy(cols_hbm, col_tables, load_sem.at[2]),
        pltpu.make_async_copy(psf_hbm, psf_tables, load_sem.at[3]),
    ]
    for load in lists + loads:
        load.start()

    def entry_for(start, patch, rank):
        seen = jnp.int32(0)
        found = jnp.int32(0)
        filled = jnp.int32(0)
        for e in range(per_device):
            hit = target[start + e] == patch
            take = jnp.logical_and(hit, seen == rank)
            found = jnp.where(take, e, found)
            filled = jnp.where(take, 1, filled)
            seen = seen + hit.astype(jnp.int32)
        return found, filled

    ext[...] = jnp.zeros_like(ext)
    arrived[0, :, 0] = jnp.zeros_like(arrived[0, :, 0])
    arrived[1, :, n_visit - 1] = jnp.zeros_like(arrived[1, :, n_visit - 1])
    corners = [(-1, -1), (-1, 1), (1, -1), (1, 1)]
    barrier = pltpu.get_barrier_semaphore()
    for d in range(1, n_patch):
        pl.semaphore_signal(
            barrier, inc=1, device_id=(v, lax.rem(p + d, n_patch)), device_id_type=MESH
        )
    for d in (1, n_visit - 1):
        pl.semaphore_signal(
            barrier, inc=1, device_id=(lax.rem(v + d, n_visit), p), device_id_type=MESH
        )
    for dv, dp in corners:
        there = (lax.rem(v + dv + n_visit, n_visit), lax.rem(p + dp + n_patch, n_patch))
        pl.semaphore_signal(barrier, inc=1, device_id=there, device_id_type=MESH)

    def inside(dv, dp):
        ok = None
        for at, shift, count in ((v, dv, n_visit), (p, dp, n_patch)):
            if shift < 0:
                term = at > 0
            elif shift > 0:
                term = at < count - 1
            else:
                continue
            ok = term if ok is None else jnp.logical_and(ok, term)
        return ok

    for load in lists:
        load.wait()

    def find(s, _):
        entry_of[s] = entry_for(base, s // CAP, lax.rem(s, CAP))[0]
        return 0

    lax.fori_loop(0, boxes, find, 0)
    for load in loads:
        load.wait()

    def warp(i, _):
        image = images[i]
        table = psf_tables[psf_index[own * n_images + i]]
        at = base + i * K_OV
        first = [
            jnp.dot(row_tables[row_pick[at + j]], image, preferred_element_type=F32).astype(BF16)
            for j in range(K_OV)
        ]
        second = [
            lax.dot_general(
                first[j], col_tables[col_pick[at + j]], NT, preferred_element_type=F32
            ).astype(BF16)
            for j in range(K_OV)
        ]
        third = [
            jnp.dot(table, second[j], preferred_element_type=F32).astype(BF16)
            for j in range(K_OV)
        ]
        for j in range(K_OV):
            matched[i * K_OV + j] = lax.dot_general(
                third[j], table, NT, preferred_element_type=F32
            ).astype(BF16)
        return 0

    lax.fori_loop(0, n_images, warp, 0)

    def patch_copy(c, d):
        there = lax.rem(p + d, n_patch)
        return pltpu.make_async_remote_copy(
            src_ref=outbox.at[c, pl.ds(there * CAP, CAP)],
            dst_ref=inbox.at[c, pl.ds(p * CAP, CAP)],
            send_sem=p_send.at[c, d - 1],
            recv_sem=p_recv.at[c, d - 1],
            device_id=(v, there),
            device_id_type=MESH,
        )

    def send_patch(c):
        def fill(s, _):
            for h in range(parts):
                at = pl.multiple_of(h * rows + c * step_rows, step_rows)
                outbox[c, s, h * step_rows : (h + 1) * step_rows, :] = matched[
                    entry_of[s], pl.ds(at, step_rows), :
                ]
            return 0

        lax.fori_loop(0, boxes, fill, 0)
        for d in range(1, n_patch):
            patch_copy(c, d).start()
        inbox[c, pl.ds(p * CAP, CAP)] = outbox[c, pl.ds(p * CAP, CAP)]

    def hop(c, r, up):
        way = 0 if up else 1
        return pltpu.make_async_remote_copy(
            src_ref=sums.at[c, r],
            dst_ref=arrived.at[way, c, r],
            send_sem=v_send.at[way, c, r],
            recv_sem=v_recv.at[way, c, r],
            device_id=(v + (1 if up else -1), p),
            device_id_type=MESH,
        )

    def pass_on(c, up, add):
        for r in reversed(range(1, n_visit)) if up else range(n_visit - 1):

            @pl.when(v < r if up else v > r)
            def _():
                if add:
                    hop(c, r, up).wait_recv()
                    came = arrived[0 if up else 1, c, r].astype(F32)
                    sums[c, r] = (sums[c, r].astype(F32) + came).astype(BF16)
                hop(c, r, up).start()

    def combine(c):
        for d in range(1, n_patch):
            patch_copy(c, d).wait_recv()
        weights = mix[...].reshape(G * G * BAND, boxes * BAND)
        for h in range(parts):
            for i in range(step_rows // BAND):
                at = h * step_rows + i * BAND
                tiles = inbox[c, :, at : at + BAND, :].reshape(boxes * BAND, TS)
                total = jnp.dot(weights, tiles, preferred_element_type=F32)
                total = total.astype(BF16).reshape(G, G, BAND, TS)
                for g in range(G):
                    sums[c, g * parts + h, :, i * BAND : (i + 1) * BAND, :] = total[g]

        @pl.when(v == 0)
        def _():
            pass_on(c, True, False)

        @pl.when(v == n_visit - 1)
        def _():
            pass_on(c, False, False)

    def forward(c, near):
        low = 2 * v < n_visit

        @pl.when(jnp.logical_and(v > 0, low if near else jnp.logical_not(low)))
        def _():
            pass_on(c, True, True)

        @pl.when(jnp.logical_and(v < n_visit - 1, jnp.logical_not(low) if near else low))
        def _():
            pass_on(c, False, True)

    def column_copy(c, k):
        at = pl.multiple_of(EDGE_R + c * step_rows, 8)
        here, there = (EDGE_C, EDGE_C + width) if k == 0 else (width, 0)
        return pltpu.make_async_remote_copy(
            src_ref=ext.at[pl.ds(at, step_rows), pl.ds(here, EDGE_C)],
            dst_ref=ext.at[pl.ds(at, step_rows), pl.ds(there, EDGE_C)],
            send_sem=c_send.at[k, c],
            recv_sem=c_recv.at[k, c],
            device_id=(v, p + (-1 if k == 0 else 1)),
            device_id_type=MESH,
        )

    def span(shift, edge, length):
        if shift < 0:
            return pl.ds(edge, edge), pl.ds(edge + length, edge)
        if shift > 0:
            return pl.ds(length, edge), pl.ds(0, edge)
        return pl.ds(edge, length), pl.ds(edge, length)

    around = [(-1, 0), (1, 0)] + corners

    def row_copy(k):
        dv, dp = around[k]
        r_from, r_to = span(dv, EDGE_R, rows)
        c_from, c_to = span(dp, EDGE_C, width)
        return pltpu.make_async_remote_copy(
            src_ref=ext.at[r_from, c_from],
            dst_ref=ext.at[r_to, c_to],
            send_sem=r_send.at[k],
            recv_sem=r_recv.at[k],
            device_id=(v + dv, p + dp),
            device_id_type=MESH,
        )

    def store(c, k):
        at = pl.multiple_of(c * step_rows, step_rows)
        if k == 0:
            here = ext.at[pl.ds(pl.multiple_of(EDGE_R + at, 8), step_rows), pl.ds(EDGE_C, width)]
        else:
            here = filtered.at[pl.ds(at, step_rows)]
        out = coadd if k == 0 else detection
        return pltpu.make_async_copy(here, out.at[pl.ds(at, step_rows)], o_sem.at[k, c])

    def finish(c):
        @pl.when(v > 0)
        def _():
            hop(c, v, True).wait_recv()

        @pl.when(v < n_visit - 1)
        def _():
            hop(c, v, False).wait_recv()

        at = pl.multiple_of(c * step_rows, step_rows)
        for g in range(G):
            total = sums[c, v, g].astype(F32)
            total = total + arrived[0, c, v, g].astype(F32)
            total = total + arrived[1, c, v, g].astype(F32)
            value = total * (1.0 / (1.0 + jnp.full((1, TS), slot_weight[g])))
            ext[pl.ds(EDGE_R + at, step_rows), EDGE_C + g * TS : EDGE_C + (g + 1) * TS] = value
        store(c, 0).start()
        for k in range(2):

            @pl.when(inside(0, -1 if k == 0 else 1))
            def _():
                column_copy(c, k).start()

        for k, (dv, dp) in enumerate(around):

            @pl.when(jnp.logical_and(c == (0 if dv < 0 else STEPS - 1), inside(dv, dp)))
            def _():
                row_copy(k).start()

    def columns_in(c):
        for k in range(2):

            @pl.when(inside(0, 1 if k == 0 else -1))
            def _():
                column_copy(c, k).wait_recv()

    count = taps.shape[0]
    radius = count // 2

    def detect(c):
        def one(i, _):
            at = pl.multiple_of(c * step_rows + i * BAND, BAND)
            held = ext[pl.ds(at, BAND + 2 * EDGE_R), :]
            low = EDGE_R - radius
            across = taps[0] * held[low : low + BAND, :]
            for j in range(1, count):
                across = across + taps[j] * held[low + j : low + j + BAND, :]
            low = EDGE_C - radius
            result = taps[0] * across[:, low : low + width]
            for j in range(1, count):
                result = result + taps[j] * across[:, low + j : low + j + width]
            filtered[pl.ds(at, BAND), :] = result
            return 0

        lax.fori_loop(0, step_rows // BAND, one, 0)
        store(c, 1).start()

    pl.semaphore_wait(barrier, n_patch - 1 + 2 + len(corners))
    for c in range(AHEAD):
        send_patch(c)

    lanes = lax.broadcasted_iota(jnp.int32, (BAND, boxes * BAND), 1)
    sublanes = lax.broadcasted_iota(jnp.int32, (BAND, boxes * BAND), 0)
    diagonal = lax.rem(lanes, BAND) == sublanes
    lane_box = lanes // BAND

    def gather(b, carry):
        slots, weights = carry
        start = (v * n_patch + b // CAP) * per_device
        entry, filled = entry_for(start, p, lax.rem(b, CAP))
        value = jnp.where(filled > 0, weight[(start + entry) // K_OV], 0.0)
        here = lane_box == b
        return (
            jnp.where(here, slot[start + entry], slots),
            jnp.where(here, value, weights),
        )

    slots, weights = lax.fori_loop(
        0,
        boxes,
        gather,
        (jnp.zeros(lanes.shape, jnp.int32), jnp.zeros(lanes.shape, F32)),
    )

    def place(s, _):
        full = jnp.where(jnp.logical_and(slots == s, diagonal), weights, 0.0)
        mix[s] = full.astype(BF16)
        return 0

    lax.fori_loop(0, G * G, place, 0)

    tile_row = (v * rows) // TS

    def tally(i, carry):
        carry = list(carry)
        for j in range(K_OV):
            e = i * K_OV + j
            at = jnp.where(target[e] == p, slot[e] - tile_row * G, -1)
            for g in range(G):
                carry[g] = carry[g] + jnp.where(at == g, weight[i], 0.0)
        return tuple(carry)

    def count_weights(k):
        half = weight.shape[0] // 2
        totals = tuple(jnp.float32(0) if k == 0 else slot_weight[g] for g in range(G))
        totals = lax.fori_loop(k * half, (k + 1) * half, tally, totals)
        for g in range(G):
            slot_weight[g] = totals[g]

    def stage(t, first, last, do):
        @pl.when(jnp.logical_and(t >= first, t <= last))
        def _():
            do()

    lag = jnp.where(jnp.logical_or(v == 0, v == n_visit - 1), LAG, 2)

    def step(t, _):
        stage(t, 0, STEPS - 1 - AHEAD, lambda: send_patch(t + AHEAD))
        stage(t, 0, STEPS - 1, lambda: combine(t))
        stage(t, 1, STEPS, lambda: forward(t - 1, True))
        stage(t, 2, STEPS + 1, lambda: forward(t - 2, False))
        stage(t, 0, 0, lambda: count_weights(0))
        stage(t, 1, 1, lambda: count_weights(1))
        stage(t, lag, STEPS + lag - 1, lambda: finish(t - lag))
        stage(t, lag + 1, STEPS + lag, lambda: columns_in(t - lag - 1))
        stage(t, lag + 3, STEPS + lag, lambda: detect(t - lag - 2))
        return 0

    lax.fori_loop(0, STEPS + LAG + 1, step, 0)
    for edge, last in ((-1, STEPS - 1), (1, 0)):
        for k, (dv, dp) in enumerate(around):
            if dv == edge:

                @pl.when(inside(-dv, -dp))
                def _():
                    row_copy(k).wait_recv()

        detect(last)

    for k, (dv, dp) in enumerate(around):

        @pl.when(inside(dv, dp))
        def _():
            row_copy(k).wait_send()

    def drain(c, _):
        for d in range(1, n_patch):
            patch_copy(c, d).wait_send()
        for k in range(2):
            store(c, k).wait()
        for k in range(2):

            @pl.when(inside(0, -1 if k == 0 else 1))
            def _():
                column_copy(c, k).wait_send()

        for r in range(n_visit):

            @pl.when(jnp.logical_and(v < r, v < n_visit - 1))
            def _():
                hop(c, r, True).wait_send()

            @pl.when(jnp.logical_and(v > r, v > 0))
            def _():
                hop(c, r, False).wait_send()

        return 0

    lax.fori_loop(0, STEPS, drain, 0)


def body(
    ccd_images,
    ccd_weight,
    psf_index,
    patch_target,
    tile_slot,
    row_matrix,
    col_matrix,
    warp_rows,
    warp_cols,
    psf_match,
    detect_kernel,
):
    n_visit = lax.axis_size("visit")
    n_patch = lax.axis_size("patch")
    rows = G * TS // n_visit
    width = G * TS
    step_rows = rows // STEPS
    high = TS // rows * step_rows
    boxes = n_patch * CAP
    smem = pl.BlockSpec(memory_space=pltpu.SMEM)
    hbm = pl.BlockSpec(memory_space=pl.ANY)
    out = jax.ShapeDtypeStruct((rows, width), F32)
    return pl.pallas_call(
        functools.partial(kernel, n_visit, n_patch),
        out_shape=(out, out),
        in_specs=[hbm] * 4 + [smem] + [hbm] * 6,
        out_specs=(hbm, hbm),
        scratch_shapes=[
            pltpu.SMEM(ccd_weight.shape, F32),
            pltpu.SMEM(psf_index.shape, jnp.int32),
            pltpu.SMEM(tile_slot.shape, jnp.int32),
            pltpu.SMEM(tile_slot.shape, jnp.int32),
            pltpu.SMEM(row_matrix.shape, jnp.int32),
            pltpu.SMEM(col_matrix.shape, jnp.int32),
            pltpu.VMEM(ccd_images.shape, BF16),
            pltpu.VMEM(warp_rows.shape, BF16),
            pltpu.VMEM(warp_cols.shape, BF16),
            pltpu.VMEM(psf_match.shape, BF16),
            pltpu.VMEM((ccd_images.shape[0] * K_OV, TS, TS), BF16),
            pltpu.SMEM((boxes,), jnp.int32),
            pltpu.SMEM((G,), F32),
            pltpu.VMEM((STEPS, boxes, high, TS), BF16),
            pltpu.VMEM((STEPS, boxes, high, TS), BF16),
            pltpu.VMEM((STEPS, n_visit, G, step_rows, TS), BF16),
            pltpu.VMEM((2, STEPS, n_visit, G, step_rows, TS), BF16),
            pltpu.VMEM((G * G, BAND, boxes * BAND), BF16),
            pltpu.VMEM((rows + 2 * EDGE_R, width + 2 * EDGE_C), F32),
            pltpu.VMEM((rows, width), F32),
            pltpu.SemaphoreType.DMA((10,)),
            pltpu.SemaphoreType.DMA((2, STEPS)),
            pltpu.SemaphoreType.DMA((STEPS, n_patch - 1)),
            pltpu.SemaphoreType.DMA((STEPS, n_patch - 1)),
            pltpu.SemaphoreType.DMA((2, STEPS, n_visit)),
            pltpu.SemaphoreType.DMA((2, STEPS, n_visit)),
            pltpu.SemaphoreType.DMA((2, STEPS)),
            pltpu.SemaphoreType.DMA((2, STEPS)),
            pltpu.SemaphoreType.DMA((6,)),
            pltpu.SemaphoreType.DMA((6,)),
        ],
        compiler_params=pltpu.CompilerParams(
            collective_id=0, has_side_effects=True, vmem_limit_bytes=60 * 1024 * 1024
        ),
    )(
        ccd_images,
        warp_rows,
        warp_cols,
        psf_match,
        detect_kernel,
        ccd_weight,
        psf_index,
        patch_target[:, 0],
        tile_slot,
        row_matrix,
        col_matrix,
    )


def solution(mesh):
    in_specs = (P(("visit", "patch"), None, None), P(), P(), P(), P(), P(), P(), P(), P(), P(), P())
    out_specs = (P("visit", "patch"), P("visit", "patch"))
    return jax.shard_map(body, mesh=mesh, in_specs=in_specs, out_specs=out_specs, check_vma=False)
```
